32 devices in a mesh: section: 2 (over core), dp: 16 (over z, y, x).
Axes of the slice: x: 2, y: 2, z: 4, core: 2. Of those that a mesh axis runs over, the one named last changes fastest.
Arguments:
- x_in: bfloat16 [2, 2048, 5120], P('section', 'dp'), may hold values from -8 to 8
- top_grad: bfloat16 [2048, 5120], P('dp'), may hold values from -6 to 6
- norm_gain: bfloat16 [2, 5120], P('section'), may hold values from 0.25 to 1.75
- proj_in: bfloat16 [2, 5120, 384], P('section', 'dp'), may hold values from -1 to 1
- proj_out: bfloat16 [2, 128, 5120], P('section', None, 'dp'), may hold values from -0.5 to 0.5
- key_cache: bfloat16 [2, 4608, 128], P('section', 'dp'), may hold values from -6 to 6
- value_cache: bfloat16 [2, 4608, 128], P('section', 'dp'), may hold values from -6 to 6
- prefix_len: int32 [16], P('dp'), may hold values from 72 to 288, as said below
- early_out: bfloat16 [2, 512, 128], P('section', 'dp'), may hold values from -0.59765625 to 0.59765625
- early_dy: bfloat16 [2, 512, 5120], P('section', 'dp'), may hold values from -6 to 6
Outputs:
- grad_x: bfloat16 [2, 2048, 5120], P('section', 'dp')
- key_cache_grad: bfloat16 [2, 4608, 128], P('section', 'dp')
- value_cache_grad: bfloat16 [2, 4608, 128], P('section', 'dp')
- wo_grad: float32 [2, 128, 5120], P('section', None, 'dp')
The draws below stay inside these ranges and needn't reach their ends.
Inputs may be any that keep to these rules, and one draw needn't show every extreme that they name: `prefix_len`: some sequence has all 288 cached positions.
All inputs are finite; a program needn't handle non-finite values.
Results may differ from the reference program's by a relative error of at most 0.02.
Values may be sent and summed in bfloat16 or wider, within the bound.
A program may use at most 64 MiB of HBM per device.

```python
import jax
import jax.numpy as jnp
from jax import lax

D = 5120
HD = 128
TOK = 128
EROWS = 32
PREF = 288
LAYERS = 2
SEQS = 16


def weights_in(key):
    drawn = jax.random.normal(jax.random.fold_in(key, 101), (LAYERS, D, 3 * HD), jnp.float32)
    return jnp.clip(drawn, -6.0, 6.0) * D ** (-0.5)


def draw_proj_in(key, part):
    return weights_in(key).astype(jnp.bfloat16)


def draw_x_in(key, part):
    drawn = jnp.clip(jax.random.normal(jax.random.fold_in(key, 106), (LAYERS, SEQS, TOK, D), jnp.float32), -6.0, 6.0)
    return drawn.reshape(LAYERS, SEQS * TOK, D).astype(jnp.bfloat16)


def draw_key_cache(key, part):
    full_shape = (LAYERS, SEQS, PREF, HD)
    drawn = jnp.clip(jax.random.normal(jax.random.fold_in(key, 108), full_shape, jnp.float32), -6.0, 6.0)
    return drawn.reshape(LAYERS, SEQS * PREF, HD).astype(jnp.bfloat16)


def draw_prefix_len(key, part):
    lowest = max(8, PREF // 4)
    lengths = jax.random.randint(jax.random.fold_in(key, 109), (SEQS,), lowest, PREF + 1)
    fullest = jax.random.randint(jax.random.fold_in(key, 110), (), 0, SEQS)
    return jnp.where(jnp.arange(SEQS) == fullest, PREF, lengths).astype(jnp.int32)


def spiked(entries, stream_key, source, target, shards_of, factor):
    def block_of(dim):
        return (jnp.arange(entries.shape[dim]) // (entries.shape[dim] // shards_of)).reshape((-1,) + (1,) * (entries.ndim - 1 - dim))

    near = jax.random.permutation(stream_key, shards_of)[block_of(target)]
    far = (block_of(target) + shards_of // 2) % shards_of
    return jnp.where((block_of(source) == near) | (block_of(source) == far), factor * entries, entries)


def block_levels(stream_key, dims, split, smallest, largest):
    level = 1.0
    for axis_at, blocks in split:
        steps = jax.random.uniform(jax.random.fold_in(jax.random.fold_in(stream_key, 6), axis_at), (blocks,), jnp.float32, smallest / len(split), largest / len(split))
        level = level * jnp.repeat(jnp.exp(steps), dims[axis_at] // blocks).reshape((-1,) + (1,) * (len(dims) - 1 - axis_at))
    return level


def bell_draw(own_key, dims, scale, limit, shards=(), kind=jnp.bfloat16):
    entries = jax.random.normal(own_key, dims, jnp.float32) * scale
    if len(shards) > 0:
        entries = block_levels(own_key, dims, shards, -0.22, 0.18) * entries
    return jnp.clip(entries, min=-limit, max=limit).astype(kind)


def noise_with(own_key, shape, scale, bound, split, heavy, held_as=jnp.bfloat16):
    result = scale * jax.random.normal(own_key, shape, jnp.float32)
    if split:
        result = result * block_levels(own_key, shape, split, -0.22, 0.18)
    return jnp.clip(spiked(result, jax.random.fold_in(own_key, 3), *heavy), -bound, bound).astype(held_as)


def setup_inputs(seed: int = 0) -> dict:
    arg_keys = jax.random.split(jax.random.key(seed), 11)
    x_in = draw_x_in(jax.random.fold_in(arg_keys[10], 71), 0)
    top_grad = bell_draw(arg_keys[1], (SEQS * TOK, D), 1.0, 6.0, ((0, 16),))
    norm_gain = jnp.clip(1.0 + 0.15 * jax.random.normal(arg_keys[2], (LAYERS, D), jnp.float32), 0.25, 1.75).astype(jnp.bfloat16)
    proj_in = draw_proj_in(jax.random.fold_in(arg_keys[10], 71), 0)
    proj_out = bell_draw(arg_keys[4], (LAYERS, HD, D), HD ** -0.5, 0.5, ((0, 2), (2, 16)))
    key_cache = draw_key_cache(jax.random.fold_in(arg_keys[10], 71), 0)
    value_cache = bell_draw(arg_keys[6], (LAYERS, SEQS * PREF, HD), 1.0, 6.0, ((0, 2), (1, 16)))
    prefix_len = draw_prefix_len(jax.random.fold_in(arg_keys[10], 71), 0)
    early_out = bell_draw(arg_keys[8], (LAYERS, SEQS * EROWS, HD), 0.1, 0.59765625, ((0, 2), (1, 16)))
    early_dy = noise_with(arg_keys[9], (LAYERS, SEQS * EROWS, D), 1.0, 6.0, ((0, 2), (1, 16)), (1, 2, 16, 2.0))
    return dict(x_in=x_in, top_grad=top_grad, norm_gain=norm_gain, proj_in=proj_in, proj_out=proj_out, key_cache=key_cache, value_cache=value_cache, prefix_len=prefix_len, early_out=early_out, early_dy=early_dy)


eps = 1e-06

def layer_back(x_rows, grad_in, gain_row, proj_in, proj_out, cache_keys, cache_values, length):
    head_size = proj_out.shape[0]
    group_rows = x_rows.shape[0]
    cache_rows = cache_keys.shape[0]
    score_scale = head_size ** (-0.5)
    widened = x_rows.astype(jnp.float32)
    inv_rms = lax.rsqrt(lax.optimization_barrier(jnp.mean(widened * widened, axis=1, keepdims=True)) + eps)
    gain_wide = gain_row.astype(jnp.float32)
    normed = (widened * inv_rms * gain_wide).astype(jnp.bfloat16)
    projected = jnp.dot(normed, proj_in, preferred_element_type=jnp.float32).astype(jnp.bfloat16)
    queries = projected[:, :head_size]
    all_keys = jnp.concatenate([cache_keys, projected[:, head_size:2 * head_size]], axis=0)
    all_values = jnp.concatenate([cache_values, projected[:, 2 * head_size:]], axis=0)
    column = lax.broadcasted_iota(jnp.int32, (group_rows, cache_rows + group_rows), 1)
    position = lax.broadcasted_iota(jnp.int32, (group_rows, cache_rows + group_rows), 0)
    visible = jnp.where(column < cache_rows, column < length, column - cache_rows <= position)
    scores = jnp.dot(queries, all_keys.T, preferred_element_type=jnp.float32) * score_scale
    highest = lax.optimization_barrier(jnp.max(jnp.where(visible, scores, -jnp.inf), axis=1, keepdims=True))
    weights = jnp.where(visible, jnp.exp(scores - highest), 0.0)
    prob_full = weights / lax.optimization_barrier(jnp.sum(weights, axis=1, keepdims=True))
    prob_low = prob_full.astype(jnp.bfloat16)
    attended = jnp.dot(prob_low, all_values, preferred_element_type=jnp.float32).astype(jnp.bfloat16)
    grad_out = jnp.dot(grad_in, proj_out.T, preferred_element_type=jnp.float32).astype(jnp.bfloat16)
    grad_prob = jnp.dot(grad_out, all_values.T, preferred_element_type=jnp.float32)
    row_delta = lax.optimization_barrier(jnp.sum(prob_full * grad_prob, axis=1, keepdims=True))
    grad_score = (prob_full * (grad_prob - row_delta) * score_scale).astype(jnp.bfloat16)
    grad_query = jnp.dot(grad_score, all_keys, preferred_element_type=jnp.float32)
    grad_keys = jnp.dot(grad_score.T, queries, preferred_element_type=jnp.float32)
    grad_values = jnp.dot(prob_low.T, grad_out, preferred_element_type=jnp.float32)
    grad_proj = jnp.concatenate([grad_query, grad_keys[cache_rows:], grad_values[cache_rows:]], axis=1).astype(jnp.bfloat16)
    grad_norm = jnp.dot(grad_proj, proj_in.T, preferred_element_type=jnp.float32)
    scaled = grad_norm * gain_wide
    branch = inv_rms * scaled - widened * inv_rms * inv_rms * inv_rms * lax.optimization_barrier(jnp.mean(widened * scaled, axis=1, keepdims=True))
    grad_x = (grad_in.astype(jnp.float32) + branch).astype(jnp.bfloat16)
    return (grad_x, grad_keys[:cache_rows].astype(jnp.bfloat16), grad_values[:cache_rows].astype(jnp.bfloat16), attended)

def reference(x_in, top_grad, norm_gain, proj_in, proj_out, key_cache, value_cache, prefix_len, early_out, early_dy):
    x_all = x_in.reshape(LAYERS, SEQS, TOK, D)
    keys_all = key_cache.reshape(LAYERS, SEQS, PREF, HD)
    values_all = value_cache.reshape(LAYERS, SEQS, PREF, HD)
    grad_in = top_grad.reshape(SEQS, TOK, D)
    backward_all = jax.vmap(layer_back, in_axes=(0, 0, None, None, None, 0, 0, 0))
    grad_list = [None] * LAYERS
    key_list = [None] * LAYERS
    value_list = [None] * LAYERS
    wo_list = [None] * LAYERS
    for layer_num in reversed(range(LAYERS)):
        grad_x, key_grad, value_grad, attended = backward_all(x_all[layer_num], grad_in, norm_gain[layer_num], proj_in[layer_num], proj_out[layer_num], keys_all[layer_num], values_all[layer_num], prefix_len)
        current = jnp.dot(attended.reshape(SEQS * TOK, HD).T, grad_in.reshape(SEQS * TOK, D), preferred_element_type=jnp.float32)
        earlier = jnp.dot(early_out[layer_num].T, early_dy[layer_num], preferred_element_type=jnp.float32)
        grad_list[layer_num] = grad_x.reshape(SEQS * TOK, D)
        key_list[layer_num] = key_grad.reshape(SEQS * PREF, HD)
        value_list[layer_num] = value_grad.reshape(SEQS * PREF, HD)
        wo_list[layer_num] = current + earlier
        grad_in = grad_x
    return (jnp.stack(grad_list), jnp.stack(key_list), jnp.stack(value_list), jnp.stack(wo_list))
```

```python
import functools

import jax
import jax.numpy as jnp
from jax import lax
from jax.experimental import pallas as pl
from jax.experimental.pallas import tpu as pltpu
from jax.sharding import PartitionSpec as P

eps = 1e-06
F32 = jnp.float32
BF16 = jnp.bfloat16
MESH = pl.DeviceIdType.MESH


def other(v, k, n):
    if n & (n - 1):
        return lax.rem(v + k, n)
    bit = 1
    while bit < n:
        if k & bit:
            v = v + bit - 2 * bit * lax.rem(v // bit, 2)
        bit *= 2
    return v


def dot(a, b, ca, cb):
    return lax.dot_general(a, b, (((ca,), (cb,)), ((), ())), preferred_element_type=F32)


def kernel(
    layers,
    sizes,
    x_ref,
    top_ref,
    gain_ref,
    wsh_ref,
    kc_ref,
    vc_ref,
    plen_ref,
    eo_ref,
    edy_ref,
    gx_ref,
    kg_ref,
    vg_ref,
    wo_ref,
    w,
    normed,
    gin,
    kall,
    vall,
    qk_acc,
    v_acc,
    go_acc,
    gproj,
    atte,
    wo_out,
    wo_in,
    w_send,
    w_recv,
    g_send,
    g_recv,
    o_send,
    o_recv,
):
    na, nb, nc = sizes
    dp = na * nb * nc
    sec = lax.axis_index("section")
    me = lax.axis_index("dp")
    top = layers - 1
    tok, width = x_ref.shape
    head = kc_ref.shape[1]
    cache = kc_ref.shape[0]
    kpad = kall.shape[0]
    shard = wsh_ref.shape[1]
    chunk = nc * shard
    chunks = width // chunk
    mz = me // (nb * nc)
    my = lax.rem(me // nc, nb)
    mx = lax.rem(me, nc)
    scale = head ** (-0.5)

    barrier = pltpu.get_barrier_semaphore()

    @pl.loop(1, dp)
    def _(k):
        pl.semaphore_signal(
            barrier, inc=1, device_id=(sec, lax.rem(me + k, dp)), device_id_type=MESH
        )

    @pl.when(sec > 0)
    def _():
        pl.semaphore_signal(barrier, inc=1, device_id=(sec - 1, me), device_id_type=MESH)

    @pl.when(sec < top)
    def _():
        pl.semaphore_signal(barrier, inc=1, device_id=(sec + 1, me), device_id_type=MESH)

    own_rows = pl.ds(pl.multiple_of(me * shard, 16), shard)
    w[:, own_rows, :] = wsh_ref[...]
    pl.semaphore_wait(barrier, dp - 1 + jnp.minimum(sec, 1) + jnp.minimum(top - sec, 1))

    def sid(kz, ky, kx):
        return (other(mz, kz, na) * nb + other(my, ky, nb)) * nc + other(mx, kx, nc)

    def piece(h, s, target, n):
        rows = w.at[h, pl.ds(pl.multiple_of(s * shard, 16), shard), :]
        return pltpu.make_async_remote_copy(
            src_ref=rows,
            dst_ref=rows,
            send_sem=w_send.at[h, n],
            recv_sem=w_recv.at[h, s],
            device_id=(sec, target),
            device_id_type=MESH,
        )

    counts = [0, 0]
    sent = []

    def send(h, s, to):
        copy = piece(h, s, sid(*to), counts[h])
        counts[h] += 1
        copy.start()
        sent.append(copy)

    def arrive(h, s):
        piece(h, s, lax.rem(me + 1, dp), 0).wait_recv()

    nmid = (nb, nc)
    nlast = (nc, nb)

    def at(h, kz, mid, last):
        return (kz, mid, last) if h == 0 else (kz, last, mid)

    def send_mid(h, s):
        for m in range(1, nmid[h]):
            send(h, s, at(h, 0, m, 0))

    def send_last(h, s):
        for m in range(1, nlast[h]):
            send(h, s, at(h, 0, 0, m))

    for kz in range(1, na):
        for h in range(2):
            send(h, me, (kz, 0, 0))
    for h in range(2):
        send_mid(h, me)
    for h in range(2):
        send_last(h, me)

    gin[tok:, :] = edy_ref[...]
    atte[tok:, :] = eo_ref[...]
    kall[:cache, :] = kc_ref[...]
    vall[:cache, :] = vc_ref[...]
    if kpad > cache + tok:
        kall[cache + tok :, :] = jnp.zeros((kpad - cache - tok, head), BF16)
        vall[cache + tok :, :] = jnp.zeros((kpad - cache - tok, head), BF16)
    qk_acc[...] = jnp.zeros_like(qk_acc)
    v_acc[...] = jnp.zeros_like(v_acc)
    go_acc[...] = jnp.zeros_like(go_acc)

    @pl.when(sec == top)
    def _():
        gin[:tok, :] = top_ref[...]

    def columns(c):
        return pl.ds(pl.multiple_of(c * chunk, 128), chunk)

    def squares(c, total):
        part = x_ref[:, columns(c)].astype(F32)
        return total + jnp.sum(part * part, axis=1, keepdims=True)

    total = lax.fori_loop(0, chunks, squares, jnp.zeros((tok, 1), F32))
    inv_rms = lax.rsqrt(total / width + eps)

    @pl.loop(0, chunks)
    def _(c):
        part = x_ref[:, columns(c)].astype(F32)
        gain = gain_ref[:, columns(c)].astype(F32)
        normed[:, columns(c)] = (part * inv_rms * gain).astype(BF16)

    def add_grad_out(c):
        go_acc[...] += dot(gin[:tok, columns(c)], w[1, columns(c), head:], 1, 0)

    def use(kz):
        for ky in range(nb):
            for h in range(2):
                for kx in range(nc):
                    if (kx if h == 0 else ky) > 0:
                        arrive(h, sid(kz, ky, kx))
            c = other(mz, kz, na) * nb + other(my, ky, nb)
            part = normed[:, columns(c)]
            qk_acc[...] += dot(part, w[0, columns(c), :], 1, 0)
            v_acc[...] += dot(part, w[1, columns(c), :head], 1, 0)

            @pl.when(sec == top)
            def _():
                add_grad_out(c)

    for kz in range(na):
        if kz > 0:
            for h in range(2):
                s = sid(kz, 0, 0)
                arrive(h, s)
                send_mid(h, s)
                send_last(h, s)
        for h in range(2):
            for m in range(1, nmid[h]):
                s = sid(*at(h, kz, m, 0))
                arrive(h, s)
                send_last(h, s)
        if kz > 0:
            use(kz - 1)
    use(na - 1)

    query = qk_acc[:, :head].astype(BF16)
    kall[cache : cache + tok, :] = qk_acc[:, head:].astype(BF16)
    vall[cache : cache + tok, :] = v_acc[...].astype(BF16)
    column = lax.broadcasted_iota(jnp.int32, (tok, kpad), 1)
    position = lax.broadcasted_iota(jnp.int32, (tok, kpad), 0)
    limit = jnp.where(column < cache, plen_ref[0], position + cache + 1)
    visible = column < limit
    scores = dot(query, kall[...], 1, 1) * scale
    highest = jnp.max(jnp.where(visible, scores, -jnp.inf), axis=1, keepdims=True)
    weights = jnp.where(visible, jnp.exp(scores - highest), 0.0)
    prob = weights / jnp.sum(weights, axis=1, keepdims=True)
    prob_low = prob.astype(BF16)
    atte[:tok, :] = dot(prob_low, vall[...], 1, 0).astype(BF16)

    def relay(c):
        return pltpu.make_async_remote_copy(
            src_ref=gx_ref.at[:, columns(c)],
            dst_ref=gin.at[pl.ds(0, tok), columns(c)],
            send_sem=g_send.at[c],
            recv_sem=g_recv.at[c],
            device_id=(jnp.maximum(sec - 1, 0), me),
            device_id_type=MESH,
        )

    def relay_in(c):
        return pltpu.make_async_remote_copy(
            src_ref=gx_ref.at[:, columns(c)],
            dst_ref=gin.at[pl.ds(0, tok), columns(c)],
            send_sem=g_send.at[c],
            recv_sem=g_recv.at[c],
            device_id=(jnp.minimum(sec + 1, top), me),
            device_id_type=MESH,
        )

    def share(owner, source):
        return pltpu.make_async_remote_copy(
            src_ref=wo_out.at[pl.ds(pl.multiple_of(owner * shard, 16), shard), :],
            dst_ref=wo_in.at[source],
            send_sem=o_send.at[owner],
            recv_sem=o_recv.at[source],
            device_id=(sec, owner),
            device_id_type=MESH,
        )

    def wo_chunk(c):
        both = dot(gin[:, columns(c)], atte[...], 0, 0)
        wo_out[columns(c), :] = both.astype(BF16)
        for j in range(nc):
            owner = c * nc + j

            @pl.when(owner != me)
            def _():
                share(owner, me).start()

    @pl.when(sec < top)
    def _():
        @pl.loop(0, chunks)
        def _(c):
            relay_in(c).wait_recv()
            add_grad_out(c)

            @pl.when(sec == 0)
            def _():
                wo_chunk(c)

    grad_out = go_acc[...].astype(BF16)
    grad_prob = dot(grad_out, vall[...], 1, 1)
    row_delta = jnp.sum(prob * grad_prob, axis=1, keepdims=True)
    grad_score = (prob * (grad_prob - row_delta) * scale).astype(BF16)
    grad_query = dot(grad_score, kall[...], 1, 0)
    grad_keys = dot(grad_score, query, 0, 0)
    grad_values = dot(prob_low, grad_out, 0, 0)
    kg_ref[...] = grad_keys[:cache].astype(BF16)
    vg_ref[...] = grad_values[:cache].astype(BF16)
    gproj[:, :head] = grad_query.astype(BF16)
    gproj[:, head : 2 * head] = grad_keys[cache : cache + tok].astype(BF16)
    gproj[:, 2 * head :] = grad_values[cache : cache + tok].astype(BF16)
    g_qk = gproj[:, : 2 * head]
    g_v = gproj[:, 2 * head :]
    row_sum = jnp.sum(g_qk.astype(F32) * qk_acc[...], axis=1, keepdims=True) + jnp.sum(
        g_v.astype(F32) * v_acc[...], axis=1, keepdims=True
    )
    pull = inv_rms * inv_rms * (row_sum / width)

    @pl.loop(0, chunks)
    def _(c):
        grad_norm = dot(g_qk, w[0, columns(c), :], 1, 1) + dot(g_v, w[1, columns(c), :head], 1, 1)
        scaled = grad_norm * gain_ref[:, columns(c)].astype(F32)
        branch = inv_rms * scaled - x_ref[:, columns(c)].astype(F32) * pull
        gx_ref[:, columns(c)] = (gin[:tok, columns(c)].astype(F32) + branch).astype(BF16)

        @pl.when(sec > 0)
        def _():
            relay(c).start()

    @pl.when(jnp.logical_or(sec > 0, top == 0))
    def _():
        @pl.loop(0, chunks)
        def _(c):
            wo_chunk(c)

    for copy in sent:
        copy.wait_send()

    @pl.when(sec > 0)
    def _():
        @pl.loop(0, chunks)
        def _(c):
            relay(c).wait_send()

    @pl.loop(1, dp)
    def _(k):
        share(lax.rem(me + k, dp), me).wait_send()

    @pl.loop(1, dp)
    def _(k):
        share(lax.rem(me + 1, dp), lax.rem(me + k, dp)).wait_recv()

    def gathered(k, part):
        return part + wo_in[lax.rem(me + k, dp)].astype(F32)

    part = lax.fori_loop(1, dp, gathered, wo_out[own_rows, :].astype(F32))
    wo_ref[...] = part


def body(
    layers,
    dp,
    x_in,
    top_grad,
    norm_gain,
    proj_in,
    proj_out,
    key_cache,
    value_cache,
    prefix_len,
    early_out,
    early_dy,
):
    tok, width = x_in.shape[1:]
    shard = proj_in.shape[1]
    head = proj_out.shape[1]
    cache = key_cache.shape[1]
    erows = early_out.shape[1]
    nc = 1
    while (nc * shard) % 128:
        nc *= 2
    nb = 2 if (dp // nc) % 2 == 0 else 1
    na = dp // (nc * nb)
    kpad = -(-(cache + tok) // 128) * 128
    chunks = dp // nc
    shards = jnp.stack(
        [
            proj_in[0, :, : 2 * head],
            jnp.concatenate([proj_in[0, :, 2 * head :], proj_out[0].T], axis=1),
        ]
    )
    vmem = pl.BlockSpec(memory_space=pltpu.VMEM)
    smem = pl.BlockSpec(memory_space=pltpu.SMEM)
    outs = pl.pallas_call(
        functools.partial(kernel, layers, (na, nb, nc)),
        out_shape=(
            jax.ShapeDtypeStruct((tok, width), BF16),
            jax.ShapeDtypeStruct((cache, head), BF16),
            jax.ShapeDtypeStruct((cache, head), BF16),
            jax.ShapeDtypeStruct((shard, head), F32),
        ),
        in_specs=[vmem] * 6 + [smem] + [vmem] * 2,
        out_specs=(vmem,) * 4,
        scratch_shapes=[
            pltpu.VMEM((2, width, 2 * head), BF16),
            pltpu.VMEM((tok, width), BF16),
            pltpu.VMEM((tok + erows, width), BF16),
            pltpu.VMEM((kpad, head), BF16),
            pltpu.VMEM((kpad, head), BF16),
            pltpu.VMEM((tok, 2 * head), F32),
            pltpu.VMEM((tok, head), F32),
            pltpu.VMEM((tok, head), F32),
            pltpu.VMEM((tok, 3 * head), BF16),
            pltpu.VMEM((tok + erows, head), BF16),
            pltpu.VMEM((width, head), BF16),
            pltpu.VMEM((dp, shard, head), BF16),
            pltpu.SemaphoreType.DMA((2, dp)),
            pltpu.SemaphoreType.DMA((2, dp)),
            pltpu.SemaphoreType.DMA((chunks,)),
            pltpu.SemaphoreType.DMA((chunks,)),
            pltpu.SemaphoreType.DMA((dp,)),
            pltpu.SemaphoreType.DMA((dp,)),
        ],
        compiler_params=pltpu.CompilerParams(
            collective_id=0, has_side_effects=True, vmem_limit_bytes=48 * 1024 * 1024
        ),
        cost_estimate=pl.CostEstimate(
            flops=8 * tok * width * head * 4, bytes_accessed=8 * tok * width, transcendentals=0
        ),
        name="window_backward",
    )(
        x_in[0],
        top_grad,
        norm_gain,
        shards,
        key_cache[0],
        value_cache[0],
        prefix_len,
        early_out[0],
        early_dy[0],
    )
    grad_x, key_grad, value_grad, wo_grad = outs
    return grad_x[None], key_grad[None], value_grad[None], wo_grad.T[None]


def solution(mesh):
    in_specs = (
        P("section", "dp", None),
        P("dp", None),
        P("section", None),
        P("section", "dp", None),
        P("section", None, "dp"),
        P("section", "dp", None),
        P("section", "dp", None),
        P("dp"),
        P("section", "dp", None),
        P("section", "dp", None),
    )
    out_specs = (
        P("section", "dp", None),
        P("section", "dp", None),
        P("section", "dp", None),
        P("section", None, "dp"),
    )
    fn = functools.partial(body, mesh.shape["section"], mesh.shape["dp"])
    return jax.shard_map(fn, mesh=mesh, in_specs=in_specs, out_specs=out_specs, check_vma=False)
```

```python
import functools

import jax
import jax.numpy as jnp
from jax import lax
from jax.experimental import pallas as pl
from jax.experimental.pallas import tpu as pltpu
from jax.sharding import PartitionSpec as P

eps = 1e-06
F32 = jnp.float32
BF16 = jnp.bfloat16
MESH = pl.DeviceIdType.MESH


def other(v, k, n):
    if n & (n - 1):
        return lax.rem(v + k, n)
    bit = 1
    while bit < n:
        if k & bit:
            v = v + bit - 2 * bit * lax.rem(v // bit, 2)
        bit *= 2
    return v


def dot(a, b, ca, cb):
    return lax.dot_general(a, b, (((ca,), (cb,)), ((), ())), preferred_element_type=F32)


def kernel(
    layers,
    sizes,
    x_hbm,
    top_ref,
    gain_ref,
    in_ref,
    out_ref,
    kc_ref,
    vc_ref,
    plen_ref,
    eo_ref,
    edy_ref,
    gx_ref,
    kg_ref,
    vg_ref,
    wo_ref,
    w,
    x_ref,
    normed,
    gin,
    kall,
    vall,
    qk_acc,
    v_acc,
    go_acc,
    gproj,
    atte,
    wo_out,
    wo_mid,
    wo_sum,
    wo_in,
    load,
    w_send,
    w_recv,
    g_send,
    g_recv,
    m_send,
    m_recv,
    o_send,
    o_recv,
):
    na, nb, nc = sizes
    dp = na * nb * nc
    sec = lax.axis_index("section")
    me = lax.axis_index("dp")
    top = layers - 1
    tok, width = x_ref.shape
    head = kc_ref.shape[1]
    cache = kc_ref.shape[0]
    kpad = kall.shape[0]
    shard = in_ref.shape[0]
    chunk = nc * shard
    chunks = width // chunk
    mz = me // (nb * nc)
    my = lax.rem(me // nc, nb)
    mx = lax.rem(me, nc)
    scale = head ** (-0.5)

    barrier = pltpu.get_barrier_semaphore()

    @pl.loop(1, dp)
    def _(k):
        pl.semaphore_signal(
            barrier, inc=1, device_id=(sec, lax.rem(me + k, dp)), device_id_type=MESH
        )

    @pl.when(sec > 0)
    def _():
        pl.semaphore_signal(barrier, inc=1, device_id=(sec - 1, me), device_id_type=MESH)

    @pl.when(sec < top)
    def _():
        pl.semaphore_signal(barrier, inc=1, device_id=(sec + 1, me), device_id_type=MESH)

    own_rows = pl.ds(pl.multiple_of(me * shard, 16), shard)
    loads = [
        pltpu.make_async_copy(source, target, load.at[n])
        for n, (source, target) in enumerate(
            [
                (in_ref.at[:, pl.ds(0, 2 * head)], w.at[0, own_rows, :]),
                (in_ref.at[:, pl.ds(2 * head, head)], w.at[1, own_rows, pl.ds(0, head)]),
                (out_ref, w.at[1, own_rows, pl.ds(head, head)]),
                (x_hbm, x_ref),
                (kc_ref, kall.at[pl.ds(0, cache), :]),
                (vc_ref, vall.at[pl.ds(0, cache), :]),
                (eo_ref, atte.at[pl.ds(tok, eo_ref.shape[0]), :]),
                (edy_ref, gin.at[pl.ds(tok, eo_ref.shape[0]), :]),
                (top_ref, gin.at[pl.ds(0, tok), :]),
            ]
        )
    ]
    for copy in loads[:-1]:
        copy.start()

    @pl.when(sec == top)
    def _():
        loads[-1].start()

    for copy in loads[:3]:
        copy.wait()
    pl.semaphore_wait(barrier, dp - 1 + jnp.minimum(sec, 1) + jnp.minimum(top - sec, 1))

    def sid(kz, ky, kx):
        return (other(mz, kz, na) * nb + other(my, ky, nb)) * nc + other(mx, kx, nc)

    def piece(h, s, target, n):
        rows = w.at[h, pl.ds(pl.multiple_of(s * shard, 16), shard), :]
        return pltpu.make_async_remote_copy(
            src_ref=rows,
            dst_ref=rows,
            send_sem=w_send.at[h, n],
            recv_sem=w_recv.at[h, s],
            device_id=(sec, target),
            device_id_type=MESH,
        )

    counts = [0, 0]
    sent = []

    def send(h, s, to):
        copy = piece(h, s, sid(*to), counts[h])
        counts[h] += 1
        copy.start()
        sent.append(copy)

    def arrive(h, s):
        piece(h, s, lax.rem(me + 1, dp), 0).wait_recv()

    nmid = (nb, nc)
    nlast = (nc, nb)

    def at(h, kz, mid, last):
        return (kz, mid, last) if h == 0 else (kz, last, mid)

    def send_mid(h, s):
        for m in range(1, nmid[h]):
            send(h, s, at(h, 0, m, 0))

    def send_last(h, s):
        for m in range(1, nlast[h]):
            send(h, s, at(h, 0, 0, m))

    for kz in range(1, na):
        for h in range(2):
            send(h, me, (kz, 0, 0))
    for h in range(2):
        send_mid(h, me)
    for h in range(2):
        send_last(h, me)

    if kpad > cache + tok:
        kall[cache + tok :, :] = jnp.zeros((kpad - cache - tok, head), BF16)
        vall[cache + tok :, :] = jnp.zeros((kpad - cache - tok, head), BF16)
    qk_acc[...] = jnp.zeros_like(qk_acc)
    v_acc[...] = jnp.zeros_like(v_acc)
    go_acc[...] = jnp.zeros_like(go_acc)

    for copy in loads[3:-1]:
        copy.wait()

    @pl.when(sec == top)
    def _():
        loads[-1].wait()

    def columns(c):
        return pl.ds(pl.multiple_of(c * chunk, 128), chunk)

    def squares(c, total):
        part = x_ref[:, columns(c)].astype(F32)
        return total + jnp.sum(part * part, axis=1, keepdims=True)

    total = lax.fori_loop(0, chunks, squares, jnp.zeros((tok, 1), F32))
    inv_rms = lax.rsqrt(total / width + eps)

    @pl.loop(0, chunks)
    def _(c):
        part = x_ref[:, columns(c)].astype(F32)
        gain = gain_ref[:, columns(c)].astype(F32)
        normed[:, columns(c)] = (part * inv_rms * gain).astype(BF16)

    def add_grad_out(c):
        go_acc[...] += dot(gin[:tok, columns(c)], w[1, columns(c), head:], 1, 0)

    def use(kz):
        for ky in range(nb):
            for h in range(2):
                for kx in range(nc):
                    if (kx if h == 0 else ky) > 0:
                        arrive(h, sid(kz, ky, kx))
            c = other(mz, kz, na) * nb + other(my, ky, nb)
            part = normed[:, columns(c)]
            qk_acc[...] += dot(part, w[0, columns(c), :], 1, 0)
            v_acc[...] += dot(part, w[1, columns(c), :head], 1, 0)

            @pl.when(sec == top)
            def _():
                add_grad_out(c)

    for kz in range(na):
        if kz > 0:
            for h in range(2):
                s = sid(kz, 0, 0)
                arrive(h, s)
                send_mid(h, s)
                send_last(h, s)
        for h in range(2):
            for m in range(1, nmid[h]):
                s = sid(*at(h, kz, m, 0))
                arrive(h, s)
                send_last(h, s)
        if kz > 0:
            use(kz - 1)
    use(na - 1)

    query = qk_acc[:, :head].astype(BF16)
    kall[cache : cache + tok, :] = qk_acc[:, head:].astype(BF16)
    vall[cache : cache + tok, :] = v_acc[...].astype(BF16)
    column = lax.broadcasted_iota(jnp.int32, (tok, kpad), 1)
    position = lax.broadcasted_iota(jnp.int32, (tok, kpad), 0)
    limit = jnp.where(column < cache, plen_ref[0], position + cache + 1)
    visible = column < limit
    scores = dot(query, kall[...], 1, 1) * scale
    highest = jnp.max(jnp.where(visible, scores, -jnp.inf), axis=1, keepdims=True)
    weights = jnp.where(visible, jnp.exp(scores - highest), 0.0)
    prob = weights / jnp.sum(weights, axis=1, keepdims=True)
    prob_low = prob.astype(BF16)
    atte[:tok, :] = dot(prob_low, vall[...], 1, 0).astype(BF16)

    def relay(c):
        return pltpu.make_async_remote_copy(
            src_ref=gx_ref.at[:, columns(c)],
            dst_ref=gin.at[pl.ds(0, tok), columns(c)],
            send_sem=g_send.at[c],
            recv_sem=g_recv.at[c],
            device_id=(jnp.maximum(sec - 1, 0), me),
            device_id_type=MESH,
        )

    def relay_in(c):
        return pltpu.make_async_remote_copy(
            src_ref=gx_ref.at[:, columns(c)],
            dst_ref=gin.at[pl.ds(0, tok), columns(c)],
            send_sem=g_send.at[c],
            recv_sem=g_recv.at[c],
            device_id=(jnp.minimum(sec + 1, top), me),
            device_id_type=MESH,
        )

    group = me // nc

    def order(i):
        return lax.rem(group + 1 + i, chunks)

    def block(c, j):
        return pl.ds(pl.multiple_of((c * nc + j) * shard, 16), shard)

    def mid(c, j, source):
        return pltpu.make_async_remote_copy(
            src_ref=wo_out.at[block(c, j), :],
            dst_ref=wo_mid.at[c, source],
            send_sem=m_send.at[c, j],
            recv_sem=m_recv.at[c, source],
            device_id=(sec, group * nc + j),
            device_id_type=MESH,
        )

    def share(c, source):
        return pltpu.make_async_remote_copy(
            src_ref=wo_sum.at[c],
            dst_ref=wo_in.at[source],
            send_sem=o_send.at[c],
            recv_sem=o_recv.at[source],
            device_id=(sec, c * nc + mx),
            device_id_type=MESH,
        )

    def wo_chunk(c):
        both = dot(gin[:, columns(c)], atte[...], 0, 0)
        wo_out[columns(c), :] = both.astype(BF16)
        for k in range(1, nc):
            mid(c, other(mx, k, nc), mx).start()

    def wo_pass(c):
        part = wo_out[block(c, mx), :].astype(F32)
        for k in range(1, nc):
            j = other(mx, k, nc)
            mid(c, j, j).wait_recv()
            part = part + wo_mid[c, j].astype(F32)
        wo_sum[c] = part.astype(BF16)

        @pl.when(c != group)
        def _():
            share(c, group).start()

    lag = min(2, chunks)

    @pl.loop(0, chunks)
    def _(i):
        c = order(i)

        @pl.when(sec < top)
        def _():
            relay_in(c).wait_recv()
            add_grad_out(c)

        wo_chunk(c)

        @pl.when(jnp.logical_and(sec < top, i >= lag))
        def _():
            wo_pass(order(i - lag))

    grad_out = go_acc[...].astype(BF16)
    grad_prob = dot(grad_out, vall[...], 1, 1)
    row_delta = jnp.sum(prob * grad_prob, axis=1, keepdims=True)
    grad_score = (prob * (grad_prob - row_delta) * scale).astype(BF16)
    grad_query = dot(grad_score, kall[...], 1, 0)
    grad_keys = dot(grad_score, query, 0, 0)
    grad_values = dot(prob_low, grad_out, 0, 0)
    kg_ref[...] = grad_keys[:cache].astype(BF16)
    vg_ref[...] = grad_values[:cache].astype(BF16)
    gproj[:, :head] = grad_query.astype(BF16)
    gproj[:, head : 2 * head] = grad_keys[cache : cache + tok].astype(BF16)
    gproj[:, 2 * head :] = grad_values[cache : cache + tok].astype(BF16)
    g_qk = gproj[:, : 2 * head]
    g_v = gproj[:, 2 * head :]
    row_sum = jnp.sum(g_qk.astype(F32) * qk_acc[...], axis=1, keepdims=True) + jnp.sum(
        g_v.astype(F32) * v_acc[...], axis=1, keepdims=True
    )
    pull = inv_rms * inv_rms * (row_sum / width)

    @pl.when(sec < top)
    def _():
        @pl.loop(chunks - lag, chunks)
        def _(i):
            wo_pass(order(i))

    @pl.loop(0, chunks)
    def _(i):
        c = order(i)
        grad_norm = dot(g_qk, w[0, columns(c), :], 1, 1) + dot(g_v, w[1, columns(c), :head], 1, 1)
        scaled = grad_norm * gain_ref[:, columns(c)].astype(F32)
        branch = inv_rms * scaled - x_ref[:, columns(c)].astype(F32) * pull
        gx_ref[:, columns(c)] = (gin[:tok, columns(c)].astype(F32) + branch).astype(BF16)

        @pl.when(sec > 0)
        def _():
            relay(c).start()

        @pl.when(sec == top)
        def _():
            wo_pass(c)

    for copy in sent:
        copy.wait_send()

    @pl.loop(0, chunks)
    def _(c):
        @pl.when(sec > 0)
        def _():
            relay(c).wait_send()

        for k in range(1, nc):
            mid(c, other(mx, k, nc), mx).wait_send()

        @pl.when(c != group)
        def _():
            share(c, group).wait_send()

    def gathered(i, part):
        source = order(i)
        share(group, source).wait_recv()
        return part + wo_in[source].astype(F32)

    wo_ref[...] = lax.fori_loop(0, chunks - 1, gathered, wo_sum[group].astype(F32))


def results(*refs):
    sems = refs[-1]
    count = len(refs) // 2
    copies = [
        pltpu.make_async_copy(refs[n], refs[count + n], sems.at[n]) for n in range(count)
    ]
    for copy in copies:
        copy.start()
    for copy in copies:
        copy.wait()


def body(
    layers,
    dp,
    x_in,
    top_grad,
    norm_gain,
    proj_in,
    proj_out,
    key_cache,
    value_cache,
    prefix_len,
    early_out,
    early_dy,
):
    tok, width = x_in.shape[1:]
    shard = proj_in.shape[1]
    head = proj_out.shape[1]
    cache = key_cache.shape[1]
    erows = early_out.shape[1]
    nc = 1
    while (nc * shard) % 128:
        nc *= 2
    nb = 2 if (dp // nc) % 2 == 0 else 1
    na = dp // (nc * nb)
    kpad = -(-(cache + tok) // 128) * 128
    chunks = dp // nc
    vmem = pl.BlockSpec(memory_space=pltpu.VMEM)
    anywhere = pl.BlockSpec(memory_space=pltpu.HBM)
    smem = pl.BlockSpec(memory_space=pltpu.SMEM)
    outs = pl.pallas_call(
        functools.partial(kernel, layers, (na, nb, nc)),
        out_shape=(
            jax.ShapeDtypeStruct((tok, width), BF16),
            jax.ShapeDtypeStruct((cache, head), BF16),
            jax.ShapeDtypeStruct((cache, head), BF16),
            jax.ShapeDtypeStruct((shard, head), F32),
        ),
        in_specs=[anywhere] * 2 + [vmem] + [anywhere] * 4 + [smem] + [anywhere] * 2,
        out_specs=(vmem,) * 4,
        scratch_shapes=[
            pltpu.VMEM((2, width, 2 * head), BF16),
            pltpu.VMEM((tok, width), BF16),
            pltpu.VMEM((tok, width), BF16),
            pltpu.VMEM((tok + erows, width), BF16),
            pltpu.VMEM((kpad, head), BF16),
            pltpu.VMEM((kpad, head), BF16),
            pltpu.VMEM((tok, 2 * head), F32),
            pltpu.VMEM((tok, head), F32),
            pltpu.VMEM((tok, head), F32),
            pltpu.VMEM((tok, 3 * head), BF16),
            pltpu.VMEM((tok + erows, head), BF16),
            pltpu.VMEM((width, head), BF16),
            pltpu.VMEM((chunks, nc, shard, head), BF16),
            pltpu.VMEM((chunks, shard, head), BF16),
            pltpu.VMEM((chunks, shard, head), BF16),
            pltpu.SemaphoreType.DMA((9,)),
            pltpu.SemaphoreType.DMA((2, dp)),
            pltpu.SemaphoreType.DMA((2, dp)),
            pltpu.SemaphoreType.DMA((chunks,)),
            pltpu.SemaphoreType.DMA((chunks,)),
            pltpu.SemaphoreType.DMA((chunks, nc)),
            pltpu.SemaphoreType.DMA((chunks, nc)),
            pltpu.SemaphoreType.DMA((chunks,)),
            pltpu.SemaphoreType.DMA((chunks,)),
        ],
        compiler_params=pltpu.CompilerParams(
            collective_id=0, has_side_effects=True, vmem_limit_bytes=48 * 1024 * 1024
        ),
        cost_estimate=pl.CostEstimate(
            flops=8 * tok * width * head * 4, bytes_accessed=8 * tok * width, transcendentals=0
        ),
        name="window_backward",
    )(
        x_in[0],
        top_grad,
        norm_gain,
        proj_in[0],
        proj_out[0].T,
        key_cache[0],
        value_cache[0],
        prefix_len,
        early_out[0],
        early_dy[0],
    )
    grad_x, key_grad, value_grad, wo_grad = pl.pallas_call(
        results,
        out_shape=[jax.ShapeDtypeStruct(out.shape, out.dtype) for out in outs],
        in_specs=[vmem] * 4,
        out_specs=[anywhere] * 4,
        scratch_shapes=[pltpu.SemaphoreType.DMA((4,))],
        name="results",
    )(*outs)
    return grad_x[None], key_grad[None], value_grad[None], wo_grad.T[None]


def solution(mesh):
    in_specs = (
        P("section", "dp", None),
        P("dp", None),
        P("section", None),
        P("section", "dp", None),
        P("section", None, "dp"),
        P("section", "dp", None),
        P("section", "dp", None),
        P("dp"),
        P("section", "dp", None),
        P("section", "dp", None),
    )
    out_specs = (
        P("section", "dp", None),
        P("section", "dp", None),
        P("section", "dp", None),
        P("section", None, "dp"),
    )
    fn = functools.partial(body, mesh.shape["section"], mesh.shape["dp"])
    return jax.shard_map(fn, mesh=mesh, in_specs=in_specs, out_specs=out_specs, check_vma=False)
```

```python
import functools

import jax
import jax.numpy as jnp
from jax import lax
from jax.experimental import pallas as pl
from jax.experimental.pallas import tpu as pltpu
from jax.sharding import PartitionSpec as P

eps = 1e-06
F32 = jnp.float32
BF16 = jnp.bfloat16
MESH = pl.DeviceIdType.MESH


def other(v, k, n):
    if n & (n - 1):
        return lax.rem(v + k, n)
    bit = 1
    while bit < n:
        if k & bit:
            v = v + bit - 2 * bit * lax.rem(v // bit, 2)
        bit *= 2
    return v


def dot(a, b, ca, cb):
    return lax.dot_general(a, b, (((ca,), (cb,)), ((), ())), preferred_element_type=F32)


def kernel(
    layers,
    sizes,
    x_hbm,
    top_ref,
    gain_ref,
    in_ref,
    out_ref,
    kc_ref,
    vc_ref,
    plen_ref,
    eo_ref,
    edy_ref,
    gx_hbm,
    kg_hbm,
    vg_hbm,
    wo_hbm,
    w,
    inv_ref,
    gx_ref,
    kg_ref,
    vg_ref,
    wo_ref,
    x_ref,
    normed,
    gin,
    kall,
    vall,
    qk_acc,
    v_acc,
    go_acc,
    gproj,
    atte,
    wo_out,
    wo_mid,
    wo_sum,
    wo_in,
    load,
    w_send,
    w_recv,
    g_send,
    g_recv,
    m_send,
    m_recv,
    o_send,
    o_recv,
    store,
    store_gx,
    gate,
):
    na, nb, nc = sizes
    dp = na * nb * nc
    sec = lax.axis_index("section")
    me = lax.axis_index("dp")
    top = layers - 1
    tok, width = x_hbm.shape
    head = kc_ref.shape[1]
    cache = kc_ref.shape[0]
    kpad = kall.shape[0]
    shard = in_ref.shape[0]
    chunk = nc * shard
    chunks = width // chunk
    mz = me // (nb * nc)
    my = lax.rem(me // nc, nb)
    mx = lax.rem(me, nc)
    scale = head ** (-0.5)

    barrier = pltpu.get_barrier_semaphore()

    @pl.loop(1, dp)
    def _(k):
        pl.semaphore_signal(
            barrier, inc=1, device_id=(sec, lax.rem(me + k, dp)), device_id_type=MESH
        )

    @pl.when(sec > 0)
    def _():
        pl.semaphore_signal(barrier, inc=1, device_id=(sec - 1, me), device_id_type=MESH)

    @pl.when(sec < top)
    def _():
        pl.semaphore_signal(barrier, inc=1, device_id=(sec + 1, me), device_id_type=MESH)

    own_rows = pl.ds(pl.multiple_of(me * shard, 16), shard)
    loads = [
        pltpu.make_async_copy(source, target, load.at[n])
        for n, (source, target) in enumerate(
            [
                (in_ref.at[:, pl.ds(0, 2 * head)], w.at[0, own_rows, :]),
                (in_ref.at[:, pl.ds(2 * head, head)], w.at[1, own_rows, pl.ds(0, head)]),
                (out_ref, w.at[1, own_rows, pl.ds(head, head)]),
                (x_hbm, x_ref),
                (kc_ref, kall.at[pl.ds(0, cache), :]),
                (vc_ref, vall.at[pl.ds(0, cache), :]),
                (eo_ref, atte.at[pl.ds(tok, eo_ref.shape[0]), :]),
                (edy_ref, gin.at[pl.ds(tok, eo_ref.shape[0]), :]),
                (top_ref, gin.at[pl.ds(0, tok), :]),
            ]
        )
    ]
    for copy in loads[:-1]:
        copy.start()

    @pl.when(sec == top)
    def _():
        loads[-1].start()

    for copy in loads[:3]:
        copy.wait()
    pl.semaphore_wait(barrier, dp - 1 + jnp.minimum(sec, 1) + jnp.minimum(top - sec, 1))

    def sid(kz, ky, kx):
        return (other(mz, kz, na) * nb + other(my, ky, nb)) * nc + other(mx, kx, nc)

    def piece(h, s, target, n):
        rows = w.at[h, pl.ds(pl.multiple_of(s * shard, 16), shard), :]
        return pltpu.make_async_remote_copy(
            src_ref=rows,
            dst_ref=rows,
            send_sem=w_send.at[h, n],
            recv_sem=w_recv.at[h, s],
            device_id=(sec, target),
            device_id_type=MESH,
        )

    counts = [0, 0]
    sent = []

    def send(h, s, to):
        copy = piece(h, s, sid(*to), counts[h])
        counts[h] += 1
        copy.start()
        sent.append(copy)

    def arrive(h, s):
        piece(h, s, lax.rem(me + 1, dp), 0).wait_recv()

    nmid = (nb, nc)
    nlast = (nc, nb)

    def at(h, kz, mid, last):
        return (kz, mid, last) if h == 0 else (kz, last, mid)

    def send_mid(h, s):
        for m in range(1, nmid[h]):
            send(h, s, at(h, 0, m, 0))

    def send_last(h, s):
        for m in range(1, nlast[h]):
            send(h, s, at(h, 0, 0, m))

    def open_gate(n):
        @pl.when(sec > 0)
        def _():
            pl.semaphore_signal(gate.at[n], inc=1, device_id=(sec - 1, me), device_id_type=MESH)

    def pass_gate(n):
        @pl.when(sec < top)
        def _():
            pl.semaphore_wait(gate.at[n], 1)

    def first_sends():
        pass_gate(0)
        for kz in range(1, na):
            for h in range(2):
                send(h, me, (kz, 0, 0))
        pass_gate(1)
        for h in range(2):
            send_mid(h, me)
        for h in range(2):
            send_last(h, me)

    def columns(c):
        return pl.ds(pl.multiple_of(c * chunk, 128), chunk)

    def prepare():
        if kpad > cache + tok:
            kall[cache + tok :, :] = jnp.zeros((kpad - cache - tok, head), BF16)
            vall[cache + tok :, :] = jnp.zeros((kpad - cache - tok, head), BF16)
        qk_acc[...] = jnp.zeros_like(qk_acc)
        v_acc[...] = jnp.zeros_like(v_acc)
        go_acc[...] = jnp.zeros_like(go_acc)

        for copy in loads[3:-1]:
            copy.wait()

        @pl.when(sec == top)
        def _():
            loads[-1].wait()

        def squares(c, total):
            part = x_ref[:, columns(c)].astype(F32)
            return total + jnp.sum(part * part, axis=1, keepdims=True)

        total = lax.fori_loop(0, chunks, squares, jnp.zeros((tok, 1), F32))
        inv_rms = lax.rsqrt(total / width + eps)
        inv_ref[...] = jnp.broadcast_to(inv_rms, inv_ref.shape)

        @pl.loop(0, chunks)
        def _(c):
            part = x_ref[:, columns(c)].astype(F32)
            gain = gain_ref[:, columns(c)].astype(F32)
            normed[:, columns(c)] = (part * inv_rms * gain).astype(BF16)

    @pl.when(sec < top)
    def _():
        prepare()

    first_sends()

    @pl.when(sec == top)
    def _():
        prepare()

    inv_rms = inv_ref[:, :1]

    def add_grad_out(c):
        go_acc[...] += dot(gin[:tok, columns(c)], w[1, columns(c), head:], 1, 0)

    def use(kz):
        for ky in range(nb):
            for h in range(2):
                for kx in range(nc):
                    if (kx if h == 0 else ky) > 0:
                        arrive(h, sid(kz, ky, kx))
            c = other(mz, kz, na) * nb + other(my, ky, nb)
            part = normed[:, columns(c)]
            qk_acc[...] += dot(part, w[0, columns(c), :], 1, 0)
            v_acc[...] += dot(part, w[1, columns(c), :head], 1, 0)

            @pl.when(sec == top)
            def _():
                add_grad_out(c)

    def relay(c):
        return pltpu.make_async_remote_copy(
            src_ref=gx_ref.at[:, columns(c)],
            dst_ref=gin.at[pl.ds(0, tok), columns(c)],
            send_sem=g_send.at[c],
            recv_sem=g_recv.at[c],
            device_id=(jnp.maximum(sec - 1, 0), me),
            device_id_type=MESH,
        )

    def relay_in(c):
        return pltpu.make_async_remote_copy(
            src_ref=gx_ref.at[:, columns(c)],
            dst_ref=gin.at[pl.ds(0, tok), columns(c)],
            send_sem=g_send.at[c],
            recv_sem=g_recv.at[c],
            device_id=(jnp.minimum(sec + 1, top), me),
            device_id_type=MESH,
        )

    def late_grad_out(phases):
        @pl.when(sec < top)
        def _():
            for kz in phases:
                for ky in range(nb):
                    c = other(mz, kz, na) * nb + other(my, ky, nb)
                    relay_in(c).wait_recv()
                    add_grad_out(c)

    for kz in range(na):
        if kz > 0:
            for h in range(2):
                s = sid(kz, 0, 0)
                arrive(h, s)
                send_mid(h, s)
                send_last(h, s)
        if kz == na - 1:
            open_gate(0)
        for h in range(2):
            for m in range(1, nmid[h]):
                s = sid(*at(h, kz, m, 0))
                arrive(h, s)
                send_last(h, s)
        if kz > 0:
            use(kz - 1)
    open_gate(1)
    late_grad_out(range(na - 1))
    use(na - 1)
    late_grad_out([na - 1])

    query = qk_acc[:, :head].astype(BF16)
    kall[cache : cache + tok, :] = qk_acc[:, head:].astype(BF16)
    vall[cache : cache + tok, :] = v_acc[...].astype(BF16)
    column = lax.broadcasted_iota(jnp.int32, (tok, kpad), 1)
    position = lax.broadcasted_iota(jnp.int32, (tok, kpad), 0)
    limit = jnp.where(column < cache, plen_ref[0], position + cache + 1)
    visible = column < limit
    scores = dot(query, kall[...], 1, 1) * scale
    highest = jnp.max(jnp.where(visible, scores, -jnp.inf), axis=1, keepdims=True)
    weights = jnp.where(visible, jnp.exp(scores - highest), 0.0)
    prob = weights / jnp.sum(weights, axis=1, keepdims=True)
    prob_low = prob.astype(BF16)
    atte[:tok, :] = dot(prob_low, vall[...], 1, 0).astype(BF16)

    group = me // nc

    def order(i):
        return lax.rem(group + 1 + i, chunks)

    def block(c, j):
        return pl.ds(pl.multiple_of((c * nc + j) * shard, 16), shard)

    def mid(c, j, source):
        return pltpu.make_async_remote_copy(
            src_ref=wo_out.at[block(c, j), :],
            dst_ref=wo_mid.at[c, source],
            send_sem=m_send.at[c, j],
            recv_sem=m_recv.at[c, source],
            device_id=(sec, group * nc + j),
            device_id_type=MESH,
        )

    def share(c, source):
        return pltpu.make_async_remote_copy(
            src_ref=wo_sum.at[c],
            dst_ref=wo_in.at[source],
            send_sem=o_send.at[c],
            recv_sem=o_recv.at[source],
            device_id=(sec, c * nc + mx),
            device_id_type=MESH,
        )

    def wo_chunk(c):
        both = dot(gin[:, columns(c)], atte[...], 0, 0)
        wo_out[columns(c), :] = both.astype(BF16)
        for k in range(1, nc):
            mid(c, other(mx, k, nc), mx).start()

    def wo_pass(c):
        part = wo_out[block(c, mx), :].astype(F32)
        for k in range(1, nc):
            j = other(mx, k, nc)
            mid(c, j, j).wait_recv()
            part = part + wo_mid[c, j].astype(F32)
        wo_sum[c] = part.astype(BF16)

        @pl.when(c != group)
        def _():
            share(c, group).start()

    lag = min(2, chunks)

    @pl.loop(0, chunks)
    def _(i):
        c = order(i)

        wo_chunk(c)

        @pl.when(jnp.logical_and(sec < top, i >= lag))
        def _():
            wo_pass(order(i - lag))

    grad_out = go_acc[...].astype(BF16)
    grad_prob = dot(grad_out, vall[...], 1, 1)
    row_delta = jnp.sum(prob * grad_prob, axis=1, keepdims=True)
    grad_score = (prob * (grad_prob - row_delta) * scale).astype(BF16)
    grad_query = dot(grad_score, kall[...], 1, 0)
    grad_keys = dot(grad_score, query, 0, 0)
    grad_values = dot(prob_low, grad_out, 0, 0)
    kg_ref[...] = grad_keys[:cache].astype(BF16)
    vg_ref[...] = grad_values[:cache].astype(BF16)
    stores = [
        pltpu.make_async_copy(source, target, store.at[n])
        for n, (source, target) in enumerate(
            [(kg_ref, kg_hbm), (vg_ref, vg_hbm), (wo_ref, wo_hbm)]
        )
    ]
    stores[0].start()
    stores[1].start()

    def store_part(c):
        return pltpu.make_async_copy(
            gx_ref.at[:, columns(c)], gx_hbm.at[:, columns(c)], store_gx.at[c]
        )

    gproj[:, :head] = grad_query.astype(BF16)
    gproj[:, head : 2 * head] = grad_keys[cache : cache + tok].astype(BF16)
    gproj[:, 2 * head :] = grad_values[cache : cache + tok].astype(BF16)
    g_qk = gproj[:, : 2 * head]
    g_v = gproj[:, 2 * head :]
    row_sum = jnp.sum(g_qk.astype(F32) * qk_acc[...], axis=1, keepdims=True) + jnp.sum(
        g_v.astype(F32) * v_acc[...], axis=1, keepdims=True
    )
    pull = inv_rms * inv_rms * (row_sum / width)

    @pl.when(sec < top)
    def _():
        @pl.loop(chunks - lag, chunks)
        def _(i):
            wo_pass(order(i))

    @pl.loop(0, chunks)
    def _(i):
        c = order(i)
        grad_norm = dot(g_qk, w[0, columns(c), :], 1, 1) + dot(g_v, w[1, columns(c), :head], 1, 1)
        scaled = grad_norm * gain_ref[:, columns(c)].astype(F32)
        branch = inv_rms * scaled - x_ref[:, columns(c)].astype(F32) * pull
        gx_ref[:, columns(c)] = (gin[:tok, columns(c)].astype(F32) + branch).astype(BF16)

        store_part(c).start()

        @pl.when(sec > 0)
        def _():
            relay(c).start()

        @pl.when(sec == top)
        def _():
            wo_pass(c)

    for copy in sent:
        copy.wait_send()

    @pl.loop(0, chunks)
    def _(c):
        @pl.when(sec > 0)
        def _():
            relay(c).wait_send()

        for k in range(1, nc):
            mid(c, other(mx, k, nc), mx).wait_send()

        @pl.when(c != group)
        def _():
            share(c, group).wait_send()

    def gathered(i, part):
        source = order(i)
        share(group, source).wait_recv()
        return part + wo_in[source].astype(F32)

    wo_ref[...] = lax.fori_loop(0, chunks - 1, gathered, wo_sum[group].astype(F32))
    stores[2].start()

    @pl.loop(0, chunks)
    def _(c):
        store_part(c).wait()

    for copy in stores:
        copy.wait()


def results(*refs):
    sems = refs[-1]
    count = len(refs) // 2
    copies = [
        pltpu.make_async_copy(refs[n], refs[count + n], sems.at[n]) for n in range(count)
    ]
    for copy in copies:
        copy.start()
    for copy in copies:
        copy.wait()


def body(
    layers,
    dp,
    x_in,
    top_grad,
    norm_gain,
    proj_in,
    proj_out,
    key_cache,
    value_cache,
    prefix_len,
    early_out,
    early_dy,
):
    tok, width = x_in.shape[1:]
    shard = proj_in.shape[1]
    head = proj_out.shape[1]
    cache = key_cache.shape[1]
    erows = early_out.shape[1]
    nc = 1
    while (nc * shard) % 128:
        nc *= 2
    nb = 2 if (dp // nc) % 2 == 0 else 1
    na = dp // (nc * nb)
    kpad = -(-(cache + tok) // 128) * 128
    chunks = dp // nc
    vmem = pl.BlockSpec(memory_space=pltpu.VMEM)
    anywhere = pl.BlockSpec(memory_space=pltpu.HBM)
    smem = pl.BlockSpec(memory_space=pltpu.SMEM)
    outs = pl.pallas_call(
        functools.partial(kernel, layers, (na, nb, nc)),
        out_shape=(
            jax.ShapeDtypeStruct((tok, width), BF16),
            jax.ShapeDtypeStruct((cache, head), BF16),
            jax.ShapeDtypeStruct((cache, head), BF16),
            jax.ShapeDtypeStruct((shard, head), F32),
        ),
        in_specs=[anywhere] * 2 + [vmem] + [anywhere] * 4 + [smem] + [anywhere] * 2,
        out_specs=(anywhere,) * 4,
        scratch_shapes=[
            pltpu.VMEM((2, width, 2 * head), BF16),
            pltpu.VMEM((tok, 128), F32),
            pltpu.VMEM((tok, width), BF16),
            pltpu.VMEM((cache, head), BF16),
            pltpu.VMEM((cache, head), BF16),
            pltpu.VMEM((shard, head), F32),
            pltpu.VMEM((tok, width), BF16),
            pltpu.VMEM((tok, width), BF16),
            pltpu.VMEM((tok + erows, width), BF16),
            pltpu.VMEM((kpad, head), BF16),
            pltpu.VMEM((kpad, head), BF16),
            pltpu.VMEM((tok, 2 * head), F32),
            pltpu.VMEM((tok, head), F32),
            pltpu.VMEM((tok, head), F32),
            pltpu.VMEM((tok, 3 * head), BF16),
            pltpu.VMEM((tok + erows, head), BF16),
            pltpu.VMEM((width, head), BF16),
            pltpu.VMEM((chunks, nc, shard, head), BF16),
            pltpu.VMEM((chunks, shard, head), BF16),
            pltpu.VMEM((chunks, shard, head), BF16),
            pltpu.SemaphoreType.DMA((9,)),
            pltpu.SemaphoreType.DMA((2, dp)),
            pltpu.SemaphoreType.DMA((2, dp)),
            pltpu.SemaphoreType.DMA((chunks,)),
            pltpu.SemaphoreType.DMA((chunks,)),
            pltpu.SemaphoreType.DMA((chunks, nc)),
            pltpu.SemaphoreType.DMA((chunks, nc)),
            pltpu.SemaphoreType.DMA((chunks,)),
            pltpu.SemaphoreType.DMA((chunks,)),
            pltpu.SemaphoreType.DMA((3,)),
            pltpu.SemaphoreType.DMA((chunks,)),
            pltpu.SemaphoreType.REGULAR((2,)),
        ],
        compiler_params=pltpu.CompilerParams(
            collective_id=0, has_side_effects=True, vmem_limit_bytes=62 * 1024 * 1024
        ),
        cost_estimate=pl.CostEstimate(
            flops=8 * tok * width * head * 4, bytes_accessed=8 * tok * width, transcendentals=0
        ),
        name="window_backward",
    )(
        x_in[0],
        top_grad,
        norm_gain,
        proj_in[0],
        proj_out[0].T,
        key_cache[0],
        value_cache[0],
        prefix_len,
        early_out[0],
        early_dy[0],
    )
    grad_x, key_grad, value_grad, wo_grad = pl.pallas_call(
        results,
        out_shape=[jax.ShapeDtypeStruct(out.shape, out.dtype) for out in outs],
        in_specs=[anywhere] * 4,
        out_specs=[anywhere] * 4,
        scratch_shapes=[pltpu.SemaphoreType.DMA((4,))],
        compiler_params=pltpu.CompilerParams(vmem_limit_bytes=62 * 1024 * 1024),
        name="results",
    )(*outs)
    return grad_x[None], key_grad[None], value_grad[None], wo_grad.T[None]


def solution(mesh):
    in_specs = (
        P("section", "dp", None),
        P("dp", None),
        P("section", None),
        P("section", "dp", None),
        P("section", None, "dp"),
        P("section", "dp", None),
        P("section", "dp", None),
        P("dp"),
        P("section", "dp", None),
        P("section", "dp", None),
    )
    out_specs = (
        P("section", "dp", None),
        P("section", "dp", None),
        P("section", "dp", None),
        P("section", None, "dp"),
    )
    fn = functools.partial(body, mesh.shape["section"], mesh.shape["dp"])
    return jax.shard_map(fn, mesh=mesh, in_specs=in_specs, out_specs=out_specs, check_vma=False)
```

```python
import functools

import jax
import jax.numpy as jnp
from jax import lax
from jax.experimental import pallas as pl
from jax.experimental.pallas import tpu as pltpu
from jax.sharding import PartitionSpec as P

eps = 1e-06
F32 = jnp.float32
BF16 = jnp.bfloat16
MESH = pl.DeviceIdType.MESH


def other(v, k, n):
    if n & (n - 1):
        return lax.rem(v + k, n)
    bit = 1
    while bit < n:
        if k & bit:
            v = v + bit - 2 * bit * lax.rem(v // bit, 2)
        bit *= 2
    return v


def dot(a, b, ca, cb):
    return lax.dot_general(a, b, (((ca,), (cb,)), ((), ())), preferred_element_type=F32)


def kernel(
    layers,
    sizes,
    x_hbm,
    top_ref,
    gain_ref,
    in_ref,
    out_ref,
    kc_ref,
    vc_ref,
    plen_ref,
    eo_ref,
    edy_ref,
    gx_hbm,
    kg_hbm,
    vg_hbm,
    wo_hbm,
    w,
    inv_ref,
    gx_ref,
    kg_ref,
    vg_ref,
    wo_ref,
    x_ref,
    normed,
    gin,
    kall,
    vall,
    qk_acc,
    v_acc,
    go_acc,
    gproj,
    atte,
    wo_out,
    wo_mid,
    wo_sum,
    wo_in,
    load,
    w_send,
    w_recv,
    g_send,
    g_recv,
    m_send,
    m_recv,
    o_send,
    o_recv,
    store,
    store_gx,
):
    na, nb, nc = sizes
    dp = na * nb * nc
    sec = lax.axis_index("section")
    me = lax.axis_index("dp")
    top = layers - 1
    tok, width = x_hbm.shape
    head = kc_ref.shape[1]
    cache = kc_ref.shape[0]
    kpad = kall.shape[0]
    shard = in_ref.shape[0]
    chunk = nc * shard
    chunks = width // chunk
    mz = me // (nb * nc)
    my = lax.rem(me // nc, nb)
    mx = lax.rem(me, nc)
    scale = head ** (-0.5)

    barrier = pltpu.get_barrier_semaphore()

    @pl.loop(1, dp)
    def _(k):
        pl.semaphore_signal(
            barrier, inc=1, device_id=(sec, lax.rem(me + k, dp)), device_id_type=MESH
        )

    @pl.when(sec > 0)
    def _():
        pl.semaphore_signal(barrier, inc=1, device_id=(sec - 1, me), device_id_type=MESH)

    @pl.when(sec < top)
    def _():
        pl.semaphore_signal(barrier, inc=1, device_id=(sec + 1, me), device_id_type=MESH)

    own_rows = pl.ds(pl.multiple_of(me * shard, 16), shard)
    loads = [
        pltpu.make_async_copy(source, target, load.at[n])
        for n, (source, target) in enumerate(
            [
                (in_ref.at[:, pl.ds(0, 2 * head)], w.at[0, own_rows, :]),
                (in_ref.at[:, pl.ds(2 * head, head)], w.at[1, own_rows, pl.ds(0, head)]),
                (out_ref, w.at[1, own_rows, pl.ds(head, head)]),
                (x_hbm, x_ref),
                (kc_ref, kall.at[pl.ds(0, cache), :]),
                (vc_ref, vall.at[pl.ds(0, cache), :]),
                (eo_ref, atte.at[pl.ds(tok, eo_ref.shape[0]), :]),
                (edy_ref, gin.at[pl.ds(tok, eo_ref.shape[0]), :]),
                (top_ref, gin.at[pl.ds(0, tok), :]),
            ]
        )
    ]
    for copy in loads[:-1]:
        copy.start()

    @pl.when(sec == top)
    def _():
        loads[-1].start()

    for copy in loads[:3]:
        copy.wait()
    pl.semaphore_wait(barrier, dp - 1 + jnp.minimum(sec, 1) + jnp.minimum(top - sec, 1))

    def sid(kz, ky, kx):
        return (other(mz, kz, na) * nb + other(my, ky, nb)) * nc + other(mx, kx, nc)

    def piece(h, s, target, n):
        rows = w.at[h, pl.ds(pl.multiple_of(s * shard, 16), shard), :]
        return pltpu.make_async_remote_copy(
            src_ref=rows,
            dst_ref=rows,
            send_sem=w_send.at[h, n],
            recv_sem=w_recv.at[h, s],
            device_id=(sec, target),
            device_id_type=MESH,
        )

    counts = [0, 0]
    sent = []

    def send(h, s, to):
        copy = piece(h, s, sid(*to), counts[h])
        counts[h] += 1
        copy.start()
        sent.append(copy)

    def arrive(h, s):
        piece(h, s, lax.rem(me + 1, dp), 0).wait_recv()

    nmid = (nb, nc)
    nlast = (nc, nb)

    def at(h, kz, mid, last):
        return (kz, mid, last) if h == 0 else (kz, last, mid)

    def send_mid(h, s):
        for m in range(1, nmid[h]):
            send(h, s, at(h, 0, m, 0))

    def send_last(h, s):
        for m in range(1, nlast[h]):
            send(h, s, at(h, 0, 0, m))

    def first_sends():
        for kz in range(1, na):
            for h in range(2):
                send(h, me, (kz, 0, 0))
        for h in range(2):
            send_mid(h, me)
        for h in range(2):
            send_last(h, me)

    def columns(c):
        return pl.ds(pl.multiple_of(c * chunk, 128), chunk)

    def prepare():
        if kpad > cache + tok:
            kall[cache + tok :, :] = jnp.zeros((kpad - cache - tok, head), BF16)
            vall[cache + tok :, :] = jnp.zeros((kpad - cache - tok, head), BF16)
        qk_acc[...] = jnp.zeros_like(qk_acc)
        v_acc[...] = jnp.zeros_like(v_acc)
        go_acc[...] = jnp.zeros_like(go_acc)

        for copy in loads[3:-1]:
            copy.wait()

        @pl.when(sec == top)
        def _():
            loads[-1].wait()

        def squares(c, total):
            part = x_ref[:, columns(c)].astype(F32)
            return total + jnp.sum(part * part, axis=1, keepdims=True)

        total = lax.fori_loop(0, chunks, squares, jnp.zeros((tok, 1), F32))
        inv_rms = lax.rsqrt(total / width + eps)
        inv_ref[...] = jnp.broadcast_to(inv_rms, inv_ref.shape)

        @pl.loop(0, chunks)
        def _(c):
            part = x_ref[:, columns(c)].astype(F32)
            gain = gain_ref[:, columns(c)].astype(F32)
            normed[:, columns(c)] = (part * inv_rms * gain).astype(BF16)

    first_sends()
    prepare()

    inv_rms = inv_ref[:, :1]

    def add_grad_out(c):
        go_acc[...] += dot(gin[:tok, columns(c)], w[1, columns(c), head:], 1, 0)

    def use(kz):
        for ky in range(nb):
            for h in range(2):
                for kx in range(nc):
                    if (kx if h == 0 else ky) > 0:
                        arrive(h, sid(kz, ky, kx))
            c = other(mz, kz, na) * nb + other(my, ky, nb)
            part = normed[:, columns(c)]
            qk_acc[...] += dot(part, w[0, columns(c), :], 1, 0)
            v_acc[...] += dot(part, w[1, columns(c), :head], 1, 0)

            @pl.when(sec == top)
            def _():
                add_grad_out(c)

    def relay(c):
        return pltpu.make_async_remote_copy(
            src_ref=gx_ref.at[:, columns(c)],
            dst_ref=gin.at[pl.ds(0, tok), columns(c)],
            send_sem=g_send.at[c],
            recv_sem=g_recv.at[c],
            device_id=(jnp.maximum(sec - 1, 0), me),
            device_id_type=MESH,
        )

    def relay_in(c):
        return pltpu.make_async_remote_copy(
            src_ref=gx_ref.at[:, columns(c)],
            dst_ref=gin.at[pl.ds(0, tok), columns(c)],
            send_sem=g_send.at[c],
            recv_sem=g_recv.at[c],
            device_id=(jnp.minimum(sec + 1, top), me),
            device_id_type=MESH,
        )

    for kz in range(na):
        if kz > 0:
            for h in range(2):
                s = sid(kz, 0, 0)
                arrive(h, s)
                send_mid(h, s)
                send_last(h, s)
        for h in range(2):
            for m in range(1, nmid[h]):
                s = sid(*at(h, kz, m, 0))
                arrive(h, s)
                send_last(h, s)
        if kz > 0:
            use(kz - 1)
    use(na - 1)

    query = qk_acc[:, :head].astype(BF16)
    kall[cache : cache + tok, :] = qk_acc[:, head:].astype(BF16)
    vall[cache : cache + tok, :] = v_acc[...].astype(BF16)
    column = lax.broadcasted_iota(jnp.int32, (tok, kpad), 1)
    position = lax.broadcasted_iota(jnp.int32, (tok, kpad), 0)
    limit = jnp.where(column < cache, plen_ref[0], position + cache + 1)
    visible = column < limit
    scores = dot(query, kall[...], 1, 1) * scale
    highest = jnp.max(jnp.where(visible, scores, -jnp.inf), axis=1, keepdims=True)
    weights = jnp.where(visible, jnp.exp(scores - highest), 0.0)
    prob = weights / jnp.sum(weights, axis=1, keepdims=True)
    prob_low = prob.astype(BF16)
    atte[:tok, :] = dot(prob_low, vall[...], 1, 0).astype(BF16)

    group = me // nc

    def order(i):
        return lax.rem(group + 1 + i, chunks)

    def block(c, j):
        return pl.ds(pl.multiple_of((c * nc + j) * shard, 16), shard)

    def mid(c, j, source):
        return pltpu.make_async_remote_copy(
            src_ref=wo_out.at[block(c, j), :],
            dst_ref=wo_mid.at[c, source],
            send_sem=m_send.at[c, j],
            recv_sem=m_recv.at[c, source],
            device_id=(sec, group * nc + j),
            device_id_type=MESH,
        )

    def share(c, source):
        return pltpu.make_async_remote_copy(
            src_ref=wo_sum.at[c],
            dst_ref=wo_in.at[source],
            send_sem=o_send.at[c],
            recv_sem=o_recv.at[source],
            device_id=(sec, c * nc + mx),
            device_id_type=MESH,
        )

    def wo_chunk(c):
        both = dot(gin[:, columns(c)], atte[...], 0, 0)
        wo_out[columns(c), :] = both.astype(BF16)
        for k in range(1, nc):
            mid(c, other(mx, k, nc), mx).start()

    def wo_pass(c):
        part = wo_out[block(c, mx), :].astype(F32)
        for k in range(1, nc):
            j = other(mx, k, nc)
            mid(c, j, j).wait_recv()
            part = part + wo_mid[c, j].astype(F32)
        wo_sum[c] = part.astype(BF16)

        @pl.when(c != group)
        def _():
            share(c, group).start()

    lag = min(2, chunks)

    @pl.loop(0, chunks)
    def _(i):
        c = order(i)


        @pl.when(sec < top)
        def _():
            relay_in(c).wait_recv()
            add_grad_out(c)

        wo_chunk(c)

        @pl.when(jnp.logical_and(sec < top, i >= lag))
        def _():
            wo_pass(order(i - lag))

    grad_out = go_acc[...].astype(BF16)
    grad_prob = dot(grad_out, vall[...], 1, 1)
    row_delta = jnp.sum(prob * grad_prob, axis=1, keepdims=True)
    grad_score = (prob * (grad_prob - row_delta) * scale).astype(BF16)
    grad_query = dot(grad_score, kall[...], 1, 0)
    grad_keys = dot(grad_score, query, 0, 0)
    grad_values = dot(prob_low, grad_out, 0, 0)
    kg_ref[...] = grad_keys[:cache].astype(BF16)
    vg_ref[...] = grad_values[:cache].astype(BF16)
    stores = [
        pltpu.make_async_copy(source, target, store.at[n])
        for n, (source, target) in enumerate(
            [(kg_ref, kg_hbm), (vg_ref, vg_hbm), (wo_ref, wo_hbm)]
        )
    ]
    stores[0].start()
    stores[1].start()

    def store_part(c):
        return pltpu.make_async_copy(
            gx_ref.at[:, columns(c)], gx_hbm.at[:, columns(c)], store_gx.at[c]
        )

    gproj[:, :head] = grad_query.astype(BF16)
    gproj[:, head : 2 * head] = grad_keys[cache : cache + tok].astype(BF16)
    gproj[:, 2 * head :] = grad_values[cache : cache + tok].astype(BF16)
    g_qk = gproj[:, : 2 * head]
    g_v = gproj[:, 2 * head :]
    row_sum = jnp.sum(g_qk.astype(F32) * qk_acc[...], axis=1, keepdims=True) + jnp.sum(
        g_v.astype(F32) * v_acc[...], axis=1, keepdims=True
    )
    pull = inv_rms * inv_rms * (row_sum / width)

    @pl.when(sec < top)
    def _():
        @pl.loop(chunks - lag, chunks)
        def _(i):
            wo_pass(order(i))

    @pl.loop(0, chunks)
    def _(i):
        c = order(i)
        grad_norm = dot(g_qk, w[0, columns(c), :], 1, 1) + dot(g_v, w[1, columns(c), :head], 1, 1)
        scaled = grad_norm * gain_ref[:, columns(c)].astype(F32)
        branch = inv_rms * scaled - x_ref[:, columns(c)].astype(F32) * pull
        gx_ref[:, columns(c)] = (gin[:tok, columns(c)].astype(F32) + branch).astype(BF16)

        store_part(c).start()

        @pl.when(sec > 0)
        def _():
            relay(c).start()

        @pl.when(sec == top)
        def _():
            wo_pass(c)

    for copy in sent:
        copy.wait_send()

    @pl.loop(0, chunks)
    def _(c):
        @pl.when(sec > 0)
        def _():
            relay(c).wait_send()

        for k in range(1, nc):
            mid(c, other(mx, k, nc), mx).wait_send()

        @pl.when(c != group)
        def _():
            share(c, group).wait_send()

    def gathered(i, part):
        source = order(i)
        share(group, source).wait_recv()
        return part + wo_in[source].astype(F32)

    wo_ref[...] = lax.fori_loop(0, chunks - 1, gathered, wo_sum[group].astype(F32))
    stores[2].start()

    @pl.loop(0, chunks)
    def _(c):
        store_part(c).wait()

    for copy in stores:
        copy.wait()


def results(*refs):
    sems = refs[-1]
    count = len(refs) // 2
    copies = [
        pltpu.make_async_copy(refs[n], refs[count + n], sems.at[n]) for n in range(count)
    ]
    for copy in copies:
        copy.start()
    for copy in copies:
        copy.wait()


def body(
    layers,
    dp,
    x_in,
    top_grad,
    norm_gain,
    proj_in,
    proj_out,
    key_cache,
    value_cache,
    prefix_len,
    early_out,
    early_dy,
):
    tok, width = x_in.shape[1:]
    shard = proj_in.shape[1]
    head = proj_out.shape[1]
    cache = key_cache.shape[1]
    erows = early_out.shape[1]
    nc = 1
    while (nc * shard) % 128:
        nc *= 2
    nb = 2 if (dp // nc) % 2 == 0 else 1
    na = dp // (nc * nb)
    kpad = -(-(cache + tok) // 128) * 128
    chunks = dp // nc
    vmem = pl.BlockSpec(memory_space=pltpu.VMEM)
    anywhere = pl.BlockSpec(memory_space=pltpu.HBM)
    smem = pl.BlockSpec(memory_space=pltpu.SMEM)
    outs = pl.pallas_call(
        functools.partial(kernel, layers, (na, nb, nc)),
        out_shape=(
            jax.ShapeDtypeStruct((tok, width), BF16),
            jax.ShapeDtypeStruct((cache, head), BF16),
            jax.ShapeDtypeStruct((cache, head), BF16),
            jax.ShapeDtypeStruct((shard, head), F32),
        ),
        in_specs=[anywhere] * 2 + [vmem] + [anywhere] * 4 + [smem] + [anywhere] * 2,
        out_specs=(anywhere,) * 4,
        scratch_shapes=[
            pltpu.VMEM((2, width, 2 * head), BF16),
            pltpu.VMEM((tok, 128), F32),
            pltpu.VMEM((tok, width), BF16),
            pltpu.VMEM((cache, head), BF16),
            pltpu.VMEM((cache, head), BF16),
            pltpu.VMEM((shard, head), F32),
            pltpu.VMEM((tok, width), BF16),
            pltpu.VMEM((tok, width), BF16),
            pltpu.VMEM((tok + erows, width), BF16),
            pltpu.VMEM((kpad, head), BF16),
            pltpu.VMEM((kpad, head), BF16),
            pltpu.VMEM((tok, 2 * head), F32),
            pltpu.VMEM((tok, head), F32),
            pltpu.VMEM((tok, head), F32),
            pltpu.VMEM((tok, 3 * head), BF16),
            pltpu.VMEM((tok + erows, head), BF16),
            pltpu.VMEM((width, head), BF16),
            pltpu.VMEM((chunks, nc, shard, head), BF16),
            pltpu.VMEM((chunks, shard, head), BF16),
            pltpu.VMEM((chunks, shard, head), BF16),
            pltpu.SemaphoreType.DMA((9,)),
            pltpu.SemaphoreType.DMA((2, dp)),
            pltpu.SemaphoreType.DMA((2, dp)),
            pltpu.SemaphoreType.DMA((chunks,)),
            pltpu.SemaphoreType.DMA((chunks,)),
            pltpu.SemaphoreType.DMA((chunks, nc)),
            pltpu.SemaphoreType.DMA((chunks, nc)),
            pltpu.SemaphoreType.DMA((chunks,)),
            pltpu.SemaphoreType.DMA((chunks,)),
            pltpu.SemaphoreType.DMA((3,)),
            pltpu.SemaphoreType.DMA((chunks,)),
        ],
        compiler_params=pltpu.CompilerParams(
            collective_id=0, has_side_effects=True, vmem_limit_bytes=62 * 1024 * 1024
        ),
        cost_estimate=pl.CostEstimate(
            flops=8 * tok * width * head * 4, bytes_accessed=8 * tok * width, transcendentals=0
        ),
        name="window_backward",
    )(
        x_in[0],
        top_grad,
        norm_gain,
        proj_in[0],
        proj_out[0].T,
        key_cache[0],
        value_cache[0],
        prefix_len,
        early_out[0],
        early_dy[0],
    )
    grad_x, key_grad, value_grad, wo_grad = pl.pallas_call(
        results,
        out_shape=[jax.ShapeDtypeStruct(out.shape, out.dtype) for out in outs],
        in_specs=[vmem] * 4,
        out_specs=[anywhere] * 4,
        scratch_shapes=[pltpu.SemaphoreType.DMA((4,))],
        compiler_params=pltpu.CompilerParams(vmem_limit_bytes=62 * 1024 * 1024),
        name="results",
    )(*outs)
    return grad_x[None], key_grad[None], value_grad[None], wo_grad.T[None]


def solution(mesh):
    in_specs = (
        P("section", "dp", None),
        P("dp", None),
        P("section", None),
        P("section", "dp", None),
        P("section", None, "dp"),
        P("section", "dp", None),
        P("section", "dp", None),
        P("dp"),
        P("section", "dp", None),
        P("section", "dp", None),
    )
    out_specs = (
        P("section", "dp", None),
        P("section", "dp", None),
        P("section", "dp", None),
        P("section", None, "dp"),
    )
    fn = functools.partial(body, mesh.shape["section"], mesh.shape["dp"])
    return jax.shard_map(fn, mesh=mesh, in_specs=in_specs, out_specs=out_specs, check_vma=False)
```
